32 devices in a mesh: groups: 2 (over x), wide: 16 (over z, y, core).
Axes of the slice: x: 2, y: 2, z: 4, core: 2. Of those that a mesh axis runs over, the one named last changes fastest.
Arguments:
- obs_values: bfloat16 [2048, 128, 128], P(('groups', 'wide')), parts along dimension 0, may hold values from -6 to 6
- kernels: bfloat16 [2048, 32, 128], P(('groups', 'wide')), parts along dimension 0, may hold values from -0.5 to 0.5
- block_owner: int32 [2048, 1], P(('groups', 'wide')), parts along dimension 0, may hold values from 0 to 15; in each aligned block of 64 rows (0 to 63, 64 to 127, ...) at most 8 rows name the same one
- block_row: int32 [2048], P(('groups', 'wide')), parts along dimension 0, may hold values from 0 to 7
- valid_count: int32 [2048], P(('groups', 'wide')), parts along dimension 0, may hold values from 1 to 128
- enc_weight: bfloat16 [128, 512], replicated, may hold values from -0.5 to 0.5
- enc_bias: float32 [512], replicated, may hold values from -3 to 3
- conv_weight: bfloat16 [3, 512, 512], replicated, may hold values from -0.15625 to 0.15625
- cotangent: bfloat16 [256, 32, 512], P(('groups', 'wide')), parts along dimension 0, may hold values from -6 to 6
Outputs:
- grid_out: bfloat16 [256, 32, 512], P(('groups', 'wide')), parts along dimension 0
- enc_grad: float32 [256, 512], P('groups'), parts along dimension 0
- conv_grad: float32 [6, 512, 512], P('groups'), parts along dimension 0
The draws below stay inside these ranges and needn't reach their ends.
There are 2 independent parts, one for each index of `groups`. The reference program is written for one: setup_inputs(seed, part) draws one part's arguments, and reference() takes and returns one part's arrays. A program takes and returns all parts, laid end to end along the dimension named above; an argument that names none is the same for every part. Nothing has to cross between parts.
Inputs may be any that keep to these rules, and one draw needn't show every extreme that they name: `block_owner`: among the 64 blocks of one index of wide, at most 8 name the same owner, a bound that some block reaches.
All inputs are finite; a program needn't handle non-finite values.
Results may differ from the reference program's by a relative error of at most 0.0074.
The reference program's roundings to bfloat16 on the way (of `hidden`, `contrib`, `grid`, `conv_back`, `grid_back` and `pre_back`) count: a program that leaves them out, or rounds other values in their place, can miss the bound.
Values may be sent and summed in bfloat16 or wider, within the bound.
A program may use at most 128 MiB of HBM per device.

```python
import math
import jax
import jax.numpy as jnp
import numpy as np
from jax import lax

D = 512
C_IN = 128
OBS_BLOCK = 128
LON = 32
ROWS_DEV = 8
BLK_DEV = 64
CAP = 8
LAT = 128
BLOCKS = 1024
N_WIDE = 16


def touch_ends(array, stream_key, smallest, high):
    index_at = [jax.random.randint(jax.random.fold_in(stream_key, axis), (), 0, length) for axis, length in enumerate(array.shape)]
    widest = array.shape.index(max(array.shape))
    beside = index_at[:widest] + [(index_at[widest] + 1) % array.shape[widest]] + index_at[widest + 1:]
    return array.at[tuple(index_at)].set(smallest).at[tuple(beside)].set(high)


def block_scale(own_key, shape, shards, low, high):
    loudness, own = 1.0, jax.random.fold_in(own_key, 6)
    for axis_at, shards_of in shards:
        heights = jnp.exp(jax.random.uniform(jax.random.fold_in(own, axis_at), (shards_of,), jnp.float32, low / len(shards), high / len(shards)))
        loudness = loudness * jnp.repeat(heights, shape[axis_at] // shards_of).reshape([-1 if axis == axis_at else 1 for axis in range(len(shape))])
    return loudness


def shared_out(rng, own, number, rows, number_of, top, reach, skew):
    ranking = jax.random.permutation(rng, number_of)
    crowded, ordinary = shares(number_of, rows * top, reach, skew, True), shares(number_of, rows * top, reach, skew, False)
    places = jnp.arange(number_of)

    def named(tallies, offset_by):
        used = int((tallies > 0).sum())
        fixed = max(1, used // 4)
        moved = fixed + (places - fixed + offset_by * (used - fixed)) % max(1, number_of - fixed)
        return jnp.zeros((number_of,), jnp.int32).at[ranking[jnp.where(places < fixed, places, moved)]].set(jnp.asarray(tallies, jnp.int32))

    tallies = jnp.where(number % 4 == 0, named(crowded, number // 4), named(ordinary, number - number // 4 - 1))
    mixed = jax.random.permutation(jax.random.fold_in(own, 3), number_of)
    donor, receiver = mixed[0:number_of // 2 * 2:2], mixed[1:number_of // 2 * 2:2]
    margin = jnp.minimum(tallies[donor] - 1, reach - tallies[receiver]) // 2
    margin = jnp.where((donor == ranking[0]) | (receiver == ranking[0]) | (tallies[receiver] == 0), 0, jnp.maximum(margin, 0))
    moved = jax.random.randint(jax.random.fold_in(own, 4), (number_of // 2,), 0, 1 << 20) % (margin + 1)
    tallies = tallies.at[donor].add(-moved).at[receiver].add(moved)
    items = jnp.searchsorted(jnp.cumsum(tallies), jnp.arange(rows * top), side="right").astype(jnp.int32)
    table = items.reshape(top, rows).T
    table = table[jax.random.permutation(jax.random.fold_in(own, 1), rows)]
    offset_by = jax.random.randint(jax.random.fold_in(own, 2), (rows, 1), 0, top)
    return jnp.take_along_axis(table, (jnp.arange(top)[None, :] + offset_by) % top, axis=1)


def shares(amount, total, most, lean, full):
    loads = [(1 << 20) // math.isqrt(grade ** lean) + 1 for grade in range(1, amount + 1)]
    largest = most if full else min(most, max(-(-total // amount), total * loads[0] // sum(loads)))
    least = 1 if total - largest >= amount - 1 else 0
    given, rest = [largest] + [least] * (amount - 1), total - largest - least * (amount - 1)
    while rest > 0:
        free = [i for i in range(1, amount) if given[i] < largest] or [i for i in range(1, amount) if given[i] < most]
        pool, remaining = sum([loads[i] for i in free]), rest
        for i in free:
            addition = min(most - given[i], max(1, remaining * loads[i] // pool), rest)
            given[i] = given[i] + addition
            rest = rest - addition
    return np.array(given)


def scatter_about(own_key, extent, width, limit, pieces=(), held_as=jnp.bfloat16):
    level = block_scale(own_key, extent, pieces, -0.22, 0.18) if pieces else 1.0
    values = jax.random.normal(own_key, extent, jnp.float32) * width * level
    return jnp.minimum(jnp.maximum(values, -limit), limit).astype(held_as)


def setup_inputs(seed: int = 0, part: int = 0) -> dict:
    streams_of = jax.random.split(jax.random.key(seed), 10)
    part_keys = jax.random.split(jax.random.fold_in(streams_of[9], part), 10)
    obs_values = scatter_about(part_keys[0], (BLOCKS, OBS_BLOCK, C_IN), 1.0, 6.0, ((0, 16),))
    kernels = scatter_about(part_keys[1], (BLOCKS, LON, OBS_BLOCK), OBS_BLOCK ** -0.5, 0.5, ((0, 16),))
    block_owner_keys = jax.random.split(jax.random.fold_in(part_keys[2], 1), BLOCKS // BLK_DEV)
    block_owner_turns = jax.random.permutation(jax.random.fold_in(part_keys[2], 3), BLOCKS // BLK_DEV)
    block_owner = jax.vmap(lambda own, number: shared_out(jax.random.fold_in(part_keys[2], 2), own, number, BLK_DEV, N_WIDE, 1, CAP, 2))(block_owner_keys, block_owner_turns).reshape((BLOCKS, 1))
    block_row = touch_ends(jax.random.randint(part_keys[3], (BLOCKS,), 0, ROWS_DEV), jax.random.fold_in(part_keys[3], 1), 0, ROWS_DEV - 1).astype(jnp.int32)
    valid_count = touch_ends(jax.random.randint(part_keys[4], (BLOCKS,), 1, OBS_BLOCK + 1), jax.random.fold_in(part_keys[4], 1), 1, OBS_BLOCK).astype(jnp.int32)
    enc_weight = scatter_about(streams_of[5], (C_IN, D), C_IN ** -0.5, 0.5)
    enc_bias = scatter_about(streams_of[6], (D,), 0.5, 3.0, (), jnp.float32)
    conv_weight = scatter_about(streams_of[7], (3, D, D), (3 * D) ** -0.5, 0.15625)
    cotangent = scatter_about(part_keys[8], (LAT, LON, D), 1.0, 6.0, ((0, 16),))
    return dict(obs_values=obs_values, kernels=kernels, block_owner=block_owner, block_row=block_row, valid_count=valid_count, enc_weight=enc_weight, enc_bias=enc_bias, conv_weight=conv_weight, cotangent=cotangent)


def gelu_slope(values):
    return jax.jvp(jax.nn.gelu, (values,), (jnp.ones_like(values),))[1]

def encode_blocks(obs_values, kernels, valid_count, enc_weight, enc_bias):
    pre_act = jnp.einsum('boc,cd->bod', obs_values.astype(jnp.float32), enc_weight.astype(jnp.float32)) + enc_bias
    slot_index = lax.broadcasted_iota(jnp.int32, obs_values.shape[:2], 1)
    obs_mask = (slot_index < valid_count[:, None].astype(jnp.int32)).astype(jnp.float32)
    hidden = (jax.nn.gelu(pre_act) * obs_mask[:, :, None]).astype(jnp.bfloat16)
    contrib = jnp.einsum('bto,bod->btd', kernels.astype(jnp.float32), hidden.astype(jnp.float32)).astype(jnp.bfloat16)
    return (contrib, pre_act, obs_mask)

def encoder_grad(obs_values, kernels, pre_act, obs_mask, tile_grad):
    hidden_back = jnp.einsum('bto,btd->bod', kernels.astype(jnp.float32), tile_grad.astype(jnp.float32))
    pre_back = (hidden_back * obs_mask[:, :, None] * gelu_slope(pre_act)).astype(jnp.bfloat16)
    return jnp.einsum('boc,bod->cd', obs_values.astype(jnp.float32), pre_back.astype(jnp.float32))

def flat_dot(left, right):
    shaped = left.reshape(-1, left.shape[-1])
    return jnp.dot(shaped, right, preferred_element_type=jnp.float32).reshape(left.shape[:-1] + (right.shape[-1],))

def reference(obs_values, kernels, block_owner, block_row, valid_count, enc_weight, enc_bias, conv_weight, cotangent):
    tiles = (block_owner[:, 0] * ROWS_DEV + block_row).astype(jnp.int32)
    groups_obs = obs_values.reshape(N_WIDE, BLK_DEV, OBS_BLOCK, C_IN)
    groups_kern = kernels.reshape(N_WIDE, BLK_DEV, LON, OBS_BLOCK)
    groups_count = valid_count.reshape(N_WIDE, BLK_DEV)

    def encode_group(packed):
        return encode_blocks(packed[0], packed[1], packed[2], enc_weight, enc_bias)[0]
    contrib = lax.map(encode_group, (groups_obs, groups_kern, groups_count)).reshape(BLOCKS, LON, D)
    summed = jax.ops.segment_sum(contrib.astype(jnp.float32), tiles, num_segments=LAT)
    grid = summed.astype(jnp.bfloat16)
    padded = jnp.pad(grid, ((1, 1), (0, 0), (0, 0)))
    conv_in = flat_dot(padded[:-2], conv_weight[0]) + flat_dot(padded[1:-1], conv_weight[1]) + flat_dot(padded[2:], conv_weight[2])
    grid_out = (grid.astype(jnp.float32) + jax.nn.gelu(conv_in)).astype(jnp.bfloat16)
    conv_back = (cotangent.astype(jnp.float32) * gelu_slope(conv_in)).astype(jnp.bfloat16)
    back_flat = conv_back.reshape(-1, D)
    conv_grad = jnp.stack([jnp.dot(padded[:-2].reshape(-1, D).T, back_flat, preferred_element_type=jnp.float32), jnp.dot(padded[1:-1].reshape(-1, D).T, back_flat, preferred_element_type=jnp.float32), jnp.dot(padded[2:].reshape(-1, D).T, back_flat, preferred_element_type=jnp.float32)])
    back_pad = jnp.pad(conv_back, ((1, 1), (0, 0), (0, 0)))
    grid_back = cotangent.astype(jnp.float32) + flat_dot(conv_back, conv_weight[1].T)
    grid_back = grid_back + flat_dot(back_pad[2:], conv_weight[0].T) + flat_dot(back_pad[:-2], conv_weight[2].T)
    grid_back = grid_back.astype(jnp.bfloat16)
    groups_tile = tiles.reshape(N_WIDE, BLK_DEV)

    def grad_group(total, packed):
        obs_part, kern_part, count_part, tile_part = packed
        unused, pre_act, obs_mask = encode_blocks(obs_part, kern_part, count_part, enc_weight, enc_bias)
        tile_grad = grid_back[tile_part]
        return (total + encoder_grad(obs_part, kern_part, pre_act, obs_mask, tile_grad), None)
    enc_grad, unused = lax.scan(grad_group, jnp.zeros((C_IN, D), jnp.float32), (groups_obs, groups_kern, groups_count, groups_tile))
    return (grid_out, enc_grad, conv_grad)
```

```python
import functools
import math

import jax
import jax.numpy as jnp
from jax import lax
from jax.experimental import pallas as pl
from jax.experimental.pallas import tpu as pltpu
from jax.sharding import PartitionSpec as P

F32, BF16 = jnp.float32, jnp.bfloat16
MIB = 1 << 20
ROOT = math.sqrt(2.0 / math.pi)
CUBE = 0.044715


def gelu(x):
    return 0.5 * x * (1.0 + jnp.tanh(ROOT * (x + CUBE * (x * x * x))))


def gelu_slope(x):
    square = x * x
    t = jnp.tanh(ROOT * (x + CUBE * (square * x)))
    return 0.5 * (1.0 + t) + (0.5 * x) * (1.0 - t * t) * (ROOT + (3.0 * CUBE * ROOT) * square)


def dot(left, right, contract=((1,), (0,))):
    return lax.dot_general(left, right, (contract, ((), ())), preferred_element_type=F32)


def orders(bits):
    plain = list(range(bits))
    other = [plain[0], *plain[2:3], *plain[1:2], *plain[3:]]
    return plain, other


def place_of(index, order):
    place = 0
    for bit in order:
        place = place * 2 + index // (1 << bit) % 2
    return place


def mask_of(count, slots):
    return (lax.broadcasted_iota(jnp.int32, (slots, 1), 0) < count).astype(F32)


def encode_kernel(tile_a, tile_b, count, obs, kern, weight, bias, out_a, out_b, acc_a, acc_b):
    blocks, slots, channels = obs.shape
    half = out_a.shape[-1]
    rows = acc_a.shape[0]

    @pl.loop(0, rows)
    def _(r):
        acc_a[r] = jnp.zeros(acc_a.shape[1:], F32)
        acc_b[r] = jnp.zeros(acc_b.shape[1:], F32)

    @pl.loop(0, blocks // 2)
    def _(i):
        for j in range(2):
            b = i * 2 + j
            pre = dot(obs[b], weight[...]) + bias[...]
            hidden = (gelu(pre) * mask_of(count[b], slots)).astype(BF16)
            contrib = dot(kern[b], hidden).astype(BF16).astype(F32)
            acc_a[tile_a[b]] += contrib[:, :half]
            acc_b[tile_b[b]] += contrib[:, half:]

    @pl.loop(0, rows)
    def _(r):
        out_a[r] = acc_a[r].astype(BF16)
        out_b[r] = acc_b[r].astype(BF16)


class Exchange:
    def __init__(self, order, total, me, copies):
        self.me, self.copies = me, copies
        self.partner, self.keep, self.give, self.size = [], [], [], []
        base, size = 0, total
        for bit in order:
            mine = me // (1 << bit) % 2
            size = size // 2
            self.partner.append(me + (1 - 2 * mine) * (1 << bit))
            self.keep.append(base + mine * size)
            self.give.append(base + (1 - mine) * size)
            self.size.append(size)
            base = base + mine * size
        self.pending = {}

    def region(self, ref, offset, size):
        return ref.at[pl.ds(pl.multiple_of(offset, 16), size)]

    def send(self, src, dst, k, tag):
        self.pending[(tag, k)] = self.copies(src, dst, self.partner[k])

    def start_sum(self, k, source, recv, shift=0):
        self.send(self.region(source, self.give[k] - shift, self.size[k]), recv[k], k, "s")

    def finish_sum(self, k, work, recv, shift=0):
        self.pending[("s", k)].wait_recv()
        size, start = self.size[k], self.keep[k] - shift
        step = math.gcd(size, 256)

        @pl.loop(0, size // step)
        def _(i):
            mine = pl.ds(pl.multiple_of(start + i * step, 16), step)
            got = recv[k][pl.ds(pl.multiple_of(i * step, 16), step)]
            work[mine] = (work[mine].astype(F32) + got.astype(F32)).astype(BF16)

    def start_gather(self, k, buffer):
        where = self.region(buffer, self.keep[k], self.size[k])
        self.send(where, where, k, "g")

    def finish_gather(self, k):
        self.pending[("g", k)].wait_recv()

    def drain(self):
        for copy in self.pending.values():
            copy.wait_send()


def grid_kernel(
    members,
    keep_slope,
    tile_a,
    tile_b,
    count,
    dense_a,
    dense_b,
    obs,
    kern,
    weight,
    bias,
    conv_weight,
    cotangent,
    grid_out,
    conv_out,
    enc_out,
    *scratch,
):
    scratch = list(scratch)
    bits = members.bit_length() - 1
    order_a, order_b = orders(bits)
    send_sems, recv_sems, local_sems = scratch.pop(), scratch.pop(), scratch.pop()
    work_a, work_b, gb_a, gb_b, slope, grid_pad, back_pad, cw_a, cw_b, cg_a, cg_b, ew, eg, total = scratch[:14]
    rest = scratch[14:]
    recv_a, recv_b, crecv_a, crecv_b, erecv = [rest[i * bits : (i + 1) * bits] for i in range(5)]

    blocks, slots, channels = obs.shape
    lon = kern.shape[1]
    rows, width = cotangent.shape
    half = width // 2
    me = lax.axis_index("wide")

    used = [0]

    def copies(src, dst, target):
        at = used[0]
        used[0] += 1
        copy = pltpu.make_async_remote_copy(
            src_ref=src,
            dst_ref=dst,
            send_sem=send_sems.at[at],
            recv_sem=recv_sems.at[at],
            device_id={"wide": target},
            device_id_type=pl.DeviceIdType.MESH,
        )
        copy.start()
        return copy

    after, before = lax.rem(me + 1, members), lax.rem(me + members - 1, members)
    grid_rows = members * rows
    sum_a, sum_b = Exchange(order_a, grid_rows, me, copies), Exchange(order_b, grid_rows, me, copies)
    conv_a, conv_b = Exchange(order_a, cw_a.shape[0], me, copies), Exchange(order_b, cw_b.shape[0], me, copies)
    enc = Exchange(order_a, ew.shape[0], me, copies)

    barrier = pltpu.get_barrier_semaphore()
    greeted = [before, after, *sum_a.partner]
    for peer in greeted:
        pl.semaphore_signal(barrier, inc=1, device_id={"wide": peer}, device_id_type=pl.DeviceIdType.MESH)
    pl.semaphore_wait(barrier, len(greeted))

    def slope_of(b):
        pre = dot(obs[b], weight[...]) + bias[...]
        return gelu_slope(pre) * mask_of(count[b], slots)

    def fill_slope(low, high):
        if keep_slope:

            @pl.loop(low, high)
            def _(b):
                slope[b] = slope_of(b)

    streams = ((sum_a, dense_a, work_a, recv_a, gb_a), (sum_b, dense_b, work_b, recv_b, gb_b))
    local = []
    for n, (ex, dense, work, recv, _) in enumerate(streams):
        ex.start_sum(0, dense, recv)
        local.append(
            pltpu.make_async_copy(ex.region(dense, ex.keep[0], ex.size[0]), work, local_sems.at[n])
        )
        local[-1].start()
    cuts = [blocks * k // bits for k in range(bits + 1)]
    fill_slope(cuts[0], cuts[1])
    for k in range(bits):
        for n, (ex, dense, work, recv, _) in enumerate(streams):
            shift = ex.keep[0]
            if k == 0:
                local[n].wait()
            ex.finish_sum(k, work, recv, shift)
            if k + 1 < bits:
                ex.start_sum(k + 1, work, recv, shift)
        if k + 1 < bits:
            fill_slope(cuts[k + 1], cuts[k + 2])

    own = pl.ds(lon, rows)
    for n, (ex, dense, work, recv, _) in enumerate(streams):
        mine = pl.ds(pl.multiple_of(ex.keep[-1] - ex.keep[0], 16), rows)
        grid_pad[own, n * half : (n + 1) * half] = work[mine]

    def halo(pad):
        up = copies(pad.at[pl.ds(rows, lon)], pad.at[pl.ds(0, lon)], after)
        down = copies(pad.at[pl.ds(lon, lon)], pad.at[pl.ds(lon + rows, lon)], before)
        return up, down

    def landed(pad, pair):
        for copy in pair:
            copy.wait_recv()
        first, last = pl.ds(0, lon), pl.ds(lon + rows, lon)
        nothing = jnp.zeros((lon, width), BF16)
        pad[first] = jnp.where(me == 0, nothing, pad[first])
        pad[last] = jnp.where(me == members - 1, nothing, pad[last])

    above, below = pl.ds(0, rows), pl.ds(2 * lon, rows)
    pair = halo(grid_pad)
    conv_in = dot(grid_pad[own], conv_weight[1])
    landed(grid_pad, pair)
    conv_in = conv_in + dot(grid_pad[above], conv_weight[0]) + dot(grid_pad[below], conv_weight[2])
    back_pad[own] = (cotangent[...].astype(F32) * gelu_slope(conv_in)).astype(BF16)
    pair_back = halo(back_pad)
    grid_out[...] = (grid_pad[own].astype(F32) + gelu(conv_in)).astype(BF16)
    turned = ((1,), (1,))
    grid_back = cotangent[...].astype(F32) + dot(back_pad[own], conv_weight[1], turned)
    landed(back_pad, pair_back)
    grid_back = grid_back + dot(back_pad[below], conv_weight[0], turned)
    grid_back = (grid_back + dot(back_pad[above], conv_weight[2], turned)).astype(BF16)
    for n, (ex, _, _, _, gb) in enumerate(streams):
        gb[pl.ds(pl.multiple_of(ex.keep[-1], 16), rows)] = grid_back[:, n * half : (n + 1) * half]
        ex.start_gather(bits - 1, gb)

    outer = ((0,), (0,))
    used_rows = 3 * width
    for k, place in enumerate((above, own, below)):
        term = dot(grid_pad[place], back_pad[own], outer).astype(BF16)
        cw_a[k * width : (k + 1) * width] = term[:, :half]
        cw_b[k * width : (k + 1) * width] = term[:, half:]
    if cw_a.shape[0] > used_rows:
        cw_a[used_rows:] = jnp.zeros((cw_a.shape[0] - used_rows, half), BF16)
        cw_b[used_rows:] = jnp.zeros((cw_b.shape[0] - used_rows, half), BF16)
    conv_streams = ((conv_a, cw_a, crecv_a, cg_a), (conv_b, cw_b, crecv_b, cg_b))
    for ex, cw, recv, _ in conv_streams:
        ex.start_sum(0, cw, recv)
    for k in range(bits):
        for ex, _, _, _, gb in streams:
            ex.finish_gather(bits - 1 - k)
            if k + 1 < bits:
                ex.start_gather(bits - 2 - k, gb)
        for ex, cw, recv, cg in conv_streams:
            ex.finish_sum(k, cw, recv)
            if k + 1 < bits:
                ex.start_sum(k + 1, cw, recv)
            else:
                mine = pl.ds(pl.multiple_of(ex.keep[-1], 16), ex.size[-1])
                cg[mine] = cw[mine]
                ex.start_gather(bits - 1, cg)

    total[...] = jnp.zeros_like(total)

    def encoder_steps(low, high):
        @pl.loop(low, high)
        def _(i):
            parts = []
            for j in range(2):
                b = i * 2 + j
                tile = jnp.concatenate([gb_a3[tile_a[b]], gb_b3[tile_b[b]]], axis=-1)
                hidden_back = dot(kern[b], tile, outer)
                factor = slope[b] if keep_slope else slope_of(b)
                parts.append((hidden_back * factor).astype(BF16))
            pair_obs = obs[pl.ds(i * 2, 2)].reshape(2 * slots, channels)
            total[...] += dot(pair_obs, jnp.concatenate(parts, axis=0), outer)

    gb_a3 = gb_a.reshape(grid_rows // lon, lon, half)
    gb_b3 = gb_b.reshape(grid_rows // lon, lon, half)
    cuts = [blocks // 2 * k // bits for k in range(bits + 1)]
    for k in range(bits):
        encoder_steps(cuts[k], cuts[k + 1])
        for ex, _, _, cg in conv_streams:
            ex.finish_gather(bits - 1 - k)
            if k + 1 < bits:
                ex.start_gather(bits - 2 - k, cg)
    ew[:channels] = total[:, :half].astype(BF16)
    ew[channels : 2 * channels] = total[:, half:].astype(BF16)
    if ew.shape[0] > 2 * channels:
        ew[2 * channels :] = jnp.zeros((ew.shape[0] - 2 * channels, half), BF16)
    enc.start_sum(0, ew, erecv)
    conv_out[:, :half] = cg_a[:used_rows]
    conv_out[:, half:] = cg_b[:used_rows]
    for k in range(bits):
        enc.finish_sum(k, ew, erecv)
        if k + 1 < bits:
            enc.start_sum(k + 1, ew, erecv)
    mine = pl.ds(pl.multiple_of(enc.keep[-1], 16), enc.size[-1])
    eg[mine] = ew[mine]
    for k in range(bits):
        enc.start_gather(bits - 1 - k, eg)
        enc.finish_gather(bits - 1 - k)
    enc_out[:, :half] = eg[:channels]
    enc_out[:, half:] = eg[channels : 2 * channels]
    for ex in (sum_a, sum_b, conv_a, conv_b, enc):
        ex.drain()
    for copy in pair + pair_back:
        copy.wait_send()


def local(
    obs_values, kernels, block_owner, block_row, valid_count, enc_weight, enc_bias, conv_weight, cotangent
):
    members = lax.axis_size("wide")
    bits = members.bit_length() - 1
    order_a, order_b = orders(bits)
    blocks, slots, channels = obs_values.shape
    lat_rows, lon, width = cotangent.shape
    half = width // 2
    owner = block_owner[:, 0]
    tile_a = place_of(owner, order_a) * lat_rows + block_row
    tile_b = place_of(owner, order_b) * lat_rows + block_row
    bias = enc_bias.reshape(1, width)
    lat = members * lat_rows
    smem, vmem = pl.BlockSpec(memory_space=pltpu.SMEM), pl.BlockSpec(memory_space=pltpu.VMEM)
    anywhere = pl.BlockSpec(memory_space=pl.ANY)

    dense_a, dense_b = pl.pallas_call(
        encode_kernel,
        out_shape=[jax.ShapeDtypeStruct((lat, lon, half), BF16)] * 2,
        in_specs=[smem] * 3 + [vmem] * 4,
        out_specs=[vmem] * 2,
        scratch_shapes=[pltpu.VMEM((lat, lon, half), F32)] * 2,
        compiler_params=pltpu.CompilerParams(vmem_limit_bytes=58 * MIB),
        name="encode",
    )(tile_a, tile_b, valid_count, obs_values, kernels, enc_weight, bias)

    rows = lat_rows * lon
    keep_slope = lat <= 256
    unit = 16 * members
    conv_rows = -(-3 * width // unit) * unit
    enc_rows = -(-2 * channels // unit) * unit
    grid_rows = members * rows

    def buffers(total):
        return [pltpu.VMEM((total >> (k + 1), half), BF16) for k in range(bits)]

    scratch = [
        pltpu.VMEM((grid_rows // 2, half), BF16),
        pltpu.VMEM((grid_rows // 2, half), BF16),
        pltpu.VMEM((grid_rows, half), BF16),
        pltpu.VMEM((grid_rows, half), BF16),
        pltpu.VMEM((blocks if keep_slope else 1, slots, width), F32),
        pltpu.VMEM((rows + 2 * lon, width), BF16),
        pltpu.VMEM((rows + 2 * lon, width), BF16),
        pltpu.VMEM((conv_rows, half), BF16),
        pltpu.VMEM((conv_rows, half), BF16),
        pltpu.VMEM((conv_rows, half), BF16),
        pltpu.VMEM((conv_rows, half), BF16),
        pltpu.VMEM((enc_rows, half), BF16),
        pltpu.VMEM((enc_rows, half), BF16),
        pltpu.VMEM((channels, width), F32),
        *buffers(grid_rows),
        *buffers(grid_rows),
        *buffers(conv_rows),
        *buffers(conv_rows),
        *buffers(enc_rows),
        pltpu.SemaphoreType.DMA((2,)),
        pltpu.SemaphoreType.DMA((10 * bits + 4,)),
        pltpu.SemaphoreType.DMA((10 * bits + 4,)),
    ]
    grid_out, conv_sum, enc_sum = pl.pallas_call(
        functools.partial(grid_kernel, members, keep_slope),
        out_shape=[
            jax.ShapeDtypeStruct((rows, width), BF16),
            jax.ShapeDtypeStruct((3 * width, width), BF16),
            jax.ShapeDtypeStruct((channels, width), BF16),
        ],
        in_specs=[smem] * 3 + [anywhere] * 2 + [vmem] * 6,
        out_specs=[vmem] * 3,
        scratch_shapes=scratch,
        compiler_params=pltpu.CompilerParams(
            collective_id=0, has_side_effects=True, vmem_limit_bytes=60 * MIB
        ),
        name="grid",
    )(
        tile_a,
        tile_b,
        valid_count,
        dense_a.reshape(grid_rows, half),
        dense_b.reshape(grid_rows, half),
        obs_values,
        kernels,
        enc_weight,
        bias,
        conv_weight,
        cotangent.reshape(rows, width),
    )
    return (
        grid_out.reshape(cotangent.shape),
        enc_sum.astype(F32),
        conv_sum.astype(F32).reshape(3, width, width),
    )


def solution(mesh):
    in_specs = (
        P(("groups", "wide"), None, None),
        P(("groups", "wide"), None, None),
        P(("groups", "wide"), None),
        P(("groups", "wide")),
        P(("groups", "wide")),
        P(),
        P(),
        P(),
        P(("groups", "wide"), None, None),
    )
    out_specs = (P(("groups", "wide"), None, None), P("groups", None), P("groups", None, None))
    return jax.shard_map(local, mesh=mesh, in_specs=in_specs, out_specs=out_specs, check_vma=False)
```

```python
import functools
import math

import jax
import jax.numpy as jnp
from jax import lax
from jax.experimental import pallas as pl
from jax.experimental.pallas import tpu as pltpu
from jax.sharding import PartitionSpec as P

F32, BF16 = jnp.float32, jnp.bfloat16
MIB = 1 << 20
ROOT = math.sqrt(2.0 / math.pi)
CUBE = 0.044715


def gelu(x):
    half = 0.5 * x
    return half + half * jnp.tanh(x * (ROOT + (ROOT * CUBE) * (x * x)))


def gelu_slope(x):
    square = x * x
    t = jnp.tanh(x * (ROOT + (ROOT * CUBE) * square))
    bend = x * (0.5 * ROOT + (1.5 * CUBE * ROOT) * square)
    return 0.5 + 0.5 * t + bend * (1.0 - t * t)


def dot(left, right, contract=((1,), (0,))):
    return lax.dot_general(left, right, (contract, ((), ())), preferred_element_type=F32)


def orders(bits):
    plain = list(range(bits))
    other = [plain[0], *plain[2:3], *plain[1:2], *plain[3:]]
    return plain, other


def place_of(index, order):
    place = 0
    for bit in order:
        place = place * 2 + index // (1 << bit) % 2
    return place


def live_part(kern, count):
    live = lax.broadcasted_iota(jnp.int32, kern.shape, 1) < count
    return jnp.where(live, kern, jnp.zeros_like(kern))


def encode_kernel(tile_a, tile_b, count, obs, kern, weight, bias, out_a, out_b, acc_a, acc_b):
    blocks, slots, channels = obs.shape
    half = out_a.shape[-1]
    rows = acc_a.shape[0]

    @pl.loop(0, rows)
    def _(r):
        acc_a[r] = jnp.zeros(acc_a.shape[1:], F32)
        acc_b[r] = jnp.zeros(acc_b.shape[1:], F32)

    @pl.loop(0, blocks // 2)
    def _(i):
        for j in range(2):
            b = i * 2 + j
            pre = dot(obs[b], weight[...]) + bias[...]
            hidden = gelu(pre).astype(BF16)
            contrib = dot(live_part(kern[b], count[b]), hidden).astype(BF16).astype(F32)
            acc_a[tile_a[b]] += contrib[:, :half]
            acc_b[tile_b[b]] += contrib[:, half:]

    @pl.loop(0, rows)
    def _(r):
        out_a[r] = acc_a[r].astype(BF16)
        out_b[r] = acc_b[r].astype(BF16)


class Exchange:
    def __init__(self, order, total, me, copies):
        self.me, self.copies = me, copies
        self.partner, self.keep, self.give, self.size = [], [], [], []
        base, size = 0, total
        for bit in order:
            mine = me // (1 << bit) % 2
            size = size // 2
            self.partner.append(me + (1 - 2 * mine) * (1 << bit))
            self.keep.append(base + mine * size)
            self.give.append(base + (1 - mine) * size)
            self.size.append(size)
            base = base + mine * size
        self.pending = {}

    def region(self, ref, offset, size):
        return ref.at[pl.ds(pl.multiple_of(offset, 16), size)]

    def send(self, src, dst, k, tag):
        self.pending[(tag, k)] = self.copies(src, dst, self.partner[k])

    def start_sum(self, k, source, recv, shift=0):
        self.send(self.region(source, self.give[k] - shift, self.size[k]), recv[k], k, "s")

    def start_rounded(self, source, stage, recv):
        self.add(stage, 0, [(source, self.give[0])], self.size[0])
        self.send(stage, recv[0], 0, "s")

    @staticmethod
    def add(out, at, terms, size):
        step = math.gcd(size, 256)

        @pl.loop(0, size // step)
        def _(i):
            parts = [
                ref[pl.ds(pl.multiple_of(start + i * step, 16), step)].astype(F32)
                for ref, start in terms
            ]
            place = pl.ds(pl.multiple_of(at + i * step, 16), step)
            out[place] = sum(parts[1:], parts[0]).astype(out.dtype)

    def finish_sum(self, k, source, out, recv, shift=0):
        self.pending[("s", k)].wait_recv()
        base, keep, size = self.keep[k], self.keep[k], self.size[k]
        if ("s", k) != ("s", len(self.size) - 1):
            give, keep, size = self.give[k + 1], self.keep[k + 1], self.size[k + 1]
            self.add(recv[k], give - base, [(source, give - shift), (recv[k], give - base)], size)
            self.send(self.region(recv[k], give - base, size), recv[k + 1], k + 1, "s")
        self.add(out, keep - shift, [(source, keep - shift), (recv[k], keep - base)], size)

    def start_gather(self, k, buffer):
        where = self.region(buffer, self.keep[k], self.size[k])
        self.send(where, where, k, "g")

    def finish_gather(self, k):
        self.pending[("g", k)].wait_recv()

    def drain(self):
        for copy in self.pending.values():
            copy.wait_send()


class ShortExchange:
    def __init__(self, bits, total, me, copies):
        self.copies, self.sent, self.levels = copies, [], []
        base, size = 0, total
        for low in range(0, bits, 2):
            unit, ways = 1 << low, 1 << min(2, bits - low)
            digit = me // unit % ways
            size = size // ways
            others = [lax.rem(digit + d, ways) for d in range(1, ways)]
            peers = [(other, me + (other - digit) * unit) for other in others]
            self.levels.append((base, digit, size, peers))
            base = base + digit * size
        self.base, self.size = base, size

    def peers(self):
        return [peer for level in self.levels for _, peer in level[3]]

    def sum(self, k, work, stage, recv):
        base, digit, size, peers = self.levels[k]
        Exchange.add(stage[k], 0, [(work, base)], size * (len(peers) + 1))
        pending = [
            self.copies(stage[k].at[pl.ds(pl.multiple_of(other * size, 16), size)], recv[k].at[d], peer)
            for d, (other, peer) in enumerate(peers)
        ]
        self.sent += pending
        mine = pl.ds(pl.multiple_of(base + digit * size, 16), size)
        for copy in pending:
            copy.wait_recv()
        total = work[mine]
        for d in range(len(peers)):
            total = total + recv[k][d].astype(F32)
        work[mine] = total

    def gather(self, k, buffer):
        base, digit, size, peers = self.levels[k]
        mine = buffer.at[pl.ds(pl.multiple_of(base + digit * size, 16), size)]
        pending = [self.copies(mine, mine, peer) for _, peer in peers]
        self.sent += pending
        for copy in pending:
            copy.wait_recv()

    def drain(self):
        for copy in self.sent:
            copy.wait_send()


def grid_kernel(
    members,
    keep_slope,
    tile_a,
    tile_b,
    count,
    dense_a,
    dense_b,
    obs,
    kern,
    weight,
    bias,
    conv_weight,
    cotangent,
    grid_out,
    conv_out,
    enc_out,
    *scratch,
):
    scratch = list(scratch)
    bits = members.bit_length() - 1
    order_a, order_b = orders(bits)
    send_sems, recv_sems, local_sems = scratch.pop(), scratch.pop(), scratch.pop()
    work_a, work_b, gb_a, gb_b, slope, grid_pad, back_pad, cw_a, cw_b, cs_a, cs_b, cg_a, cg_b, ew, eg, total = scratch[:16]
    acc_a, acc_b = scratch[16:18] if keep_slope else (work_a, work_b)
    rest = scratch[18:] if keep_slope else scratch[16:]
    recv_a, recv_b, crecv_a, crecv_b = [rest[i * bits : (i + 1) * bits] for i in range(4)]
    levels = (bits + 1) // 2
    estage, erecv = rest[4 * bits : 4 * bits + levels], rest[4 * bits + levels :]

    blocks, slots, channels = obs.shape
    lon = kern.shape[1]
    rows, width = cotangent.shape
    half = width // 2
    me = lax.axis_index("wide")

    used = [0]

    def copies(src, dst, target):
        at = used[0]
        used[0] += 1
        copy = pltpu.make_async_remote_copy(
            src_ref=src,
            dst_ref=dst,
            send_sem=send_sems.at[at],
            recv_sem=recv_sems.at[at],
            device_id={"wide": target},
            device_id_type=pl.DeviceIdType.MESH,
        )
        copy.start()
        return copy

    after, before = lax.rem(me + 1, members), lax.rem(me + members - 1, members)
    grid_rows = members * rows
    sum_a, sum_b = Exchange(order_a, grid_rows, me, copies), Exchange(order_b, grid_rows, me, copies)
    conv_a, conv_b = Exchange(order_a, cw_a.shape[0], me, copies), Exchange(order_b, cw_b.shape[0], me, copies)
    enc = ShortExchange(bits, ew.shape[0], me, copies)

    barrier = pltpu.get_barrier_semaphore()
    greeted = [before, after, *enc.peers()]
    for peer in greeted:
        pl.semaphore_signal(barrier, inc=1, device_id={"wide": peer}, device_id_type=pl.DeviceIdType.MESH)
    pl.semaphore_wait(barrier, len(greeted))

    def slope_of(b):
        pre = dot(obs[b], weight[...]) + bias[...]
        return gelu_slope(pre)

    def fill_slope(low, high):
        if keep_slope:

            @pl.loop(low, high)
            def _(b):
                slope[b] = slope_of(b)

    streams = ((sum_a, dense_a, work_a, recv_a, gb_a), (sum_b, dense_b, work_b, recv_b, gb_b))
    sums = (acc_a, acc_b)
    local = []
    for n, (ex, dense, work, recv, _) in enumerate(streams):
        ex.start_sum(0, dense, recv)
        local.append(
            pltpu.make_async_copy(ex.region(dense, ex.keep[0], ex.size[0]), work, local_sems.at[n])
        )
        local[-1].start()
    cuts = [blocks * k // bits for k in range(bits + 1)]
    fill_slope(cuts[0], cuts[1])
    for k in range(bits):
        for n, (ex, dense, work, recv, _) in enumerate(streams):
            shift = ex.keep[0]
            if k == 0:
                local[n].wait()
            ex.finish_sum(k, work if k == 0 else sums[n], sums[n], recv, shift)
        if k + 1 < bits:
            fill_slope(cuts[k + 1], cuts[k + 2])

    own = pl.ds(lon, rows)
    for n, (ex, dense, work, recv, _) in enumerate(streams):
        mine = pl.ds(pl.multiple_of(ex.keep[-1] - ex.keep[0], 16), rows)
        grid_pad[own, n * half : (n + 1) * half] = sums[n][mine].astype(BF16)

    def halo(pad):
        up = copies(pad.at[pl.ds(rows, lon)], pad.at[pl.ds(0, lon)], after)
        down = copies(pad.at[pl.ds(lon, lon)], pad.at[pl.ds(lon + rows, lon)], before)
        return up, down

    def landed(pad, pair):
        for copy in pair:
            copy.wait_recv()
        first, last = pl.ds(0, lon), pl.ds(lon + rows, lon)
        nothing = jnp.zeros((lon, width), BF16)
        pad[first] = jnp.where(me == 0, nothing, pad[first])
        pad[last] = jnp.where(me == members - 1, nothing, pad[last])

    above, below = pl.ds(0, rows), pl.ds(2 * lon, rows)
    pair = halo(grid_pad)
    conv_in = dot(grid_pad[own], conv_weight[1])
    landed(grid_pad, pair)
    conv_in = conv_in + dot(grid_pad[above], conv_weight[0]) + dot(grid_pad[below], conv_weight[2])
    back_pad[own] = (cotangent[...].astype(F32) * gelu_slope(conv_in)).astype(BF16)
    pair_back = halo(back_pad)
    grid_out[...] = (grid_pad[own].astype(F32) + gelu(conv_in)).astype(BF16)
    turned = ((1,), (1,))
    grid_back = cotangent[...].astype(F32) + dot(back_pad[own], conv_weight[1], turned)
    landed(back_pad, pair_back)
    grid_back = grid_back + dot(back_pad[below], conv_weight[0], turned)
    grid_back = (grid_back + dot(back_pad[above], conv_weight[2], turned)).astype(BF16)
    for n, (ex, _, _, _, gb) in enumerate(streams):
        gb[pl.ds(pl.multiple_of(ex.keep[-1], 16), rows)] = grid_back[:, n * half : (n + 1) * half]
        ex.start_gather(bits - 1, gb)

    outer = ((0,), (0,))
    used_rows = 3 * width
    for k, place in enumerate((above, own, below)):
        term = dot(grid_pad[place], back_pad[own], outer).astype(cw_a.dtype)
        cw_a[k * width : (k + 1) * width] = term[:, :half]
        cw_b[k * width : (k + 1) * width] = term[:, half:]
    if cw_a.shape[0] > used_rows:
        cw_a[used_rows:] = jnp.zeros((cw_a.shape[0] - used_rows, half), cw_a.dtype)
        cw_b[used_rows:] = jnp.zeros((cw_b.shape[0] - used_rows, half), cw_b.dtype)
    conv_streams = ((conv_a, cw_a, crecv_a, cg_a), (conv_b, cw_b, crecv_b, cg_b))
    for (ex, cw, recv, _), stage in zip(conv_streams, (cs_a, cs_b)):
        ex.start_rounded(cw, stage, recv)
    for k in range(bits):
        for ex, _, _, _, gb in streams:
            ex.finish_gather(bits - 1 - k)
            if k + 1 < bits:
                ex.start_gather(bits - 2 - k, gb)
        if k > 0:
            for ex, cw, recv, _ in conv_streams:
                ex.finish_sum(k - 1, cw, cw, recv)

    def conv_step(k):
        for ex, cw, recv, cg in conv_streams:
            if k == 0:
                ex.finish_sum(bits - 1, cw, cw, recv)
                mine = pl.ds(pl.multiple_of(ex.keep[-1], 16), ex.size[-1])
                cg[mine] = cw[mine].astype(BF16)
            else:
                ex.finish_gather(bits - k)
            if k < bits:
                ex.start_gather(bits - 1 - k, cg)

    total[...] = jnp.zeros_like(total)

    def encoder_steps(low, high):
        @pl.loop(low, high)
        def _(i):
            parts = []
            for j in range(2):
                b = i * 2 + j
                tile = jnp.concatenate([gb_a3[tile_a[b]], gb_b3[tile_b[b]]], axis=-1)
                hidden_back = dot(live_part(kern[b], count[b]), tile, outer)
                factor = slope[b] if keep_slope else slope_of(b)
                parts.append((hidden_back * factor).astype(BF16))
            pair_obs = obs[pl.ds(i * 2, 2)].reshape(2 * slots, channels)
            total[...] += dot(pair_obs, jnp.concatenate(parts, axis=0), outer)

    gb_a3 = gb_a.reshape(grid_rows // lon, lon, half)
    gb_b3 = gb_b.reshape(grid_rows // lon, lon, half)
    cuts = [blocks // 2 * k // bits for k in range(bits + 1)]
    done = 0
    for k in range(bits):
        encoder_steps(cuts[k], cuts[k + 1])
        if k in (bits // 2, bits - 1):
            conv_step(done)
            done += 1
    ew[:channels] = total[:, :half]
    ew[channels : 2 * channels] = total[:, half:]
    if ew.shape[0] > 2 * channels:
        ew[2 * channels :] = jnp.zeros((ew.shape[0] - 2 * channels, half), F32)
    for k in range(levels):
        enc.sum(k, ew, estage, erecv)
        if done <= bits:
            conv_step(done)
            done += 1
    mine = pl.ds(pl.multiple_of(enc.base, 16), enc.size)
    eg[mine] = ew[mine].astype(BF16)
    for k in range(levels):
        enc.gather(levels - 1 - k, eg)
        if done <= bits:
            conv_step(done)
            done += 1
    while done <= bits:
        conv_step(done)
        done += 1
    conv_out[:, :half] = cg_a[:used_rows]
    conv_out[:, half:] = cg_b[:used_rows]
    enc_out[:, :half] = eg[:channels]
    enc_out[:, half:] = eg[channels : 2 * channels]
    for ex in (sum_a, sum_b, conv_a, conv_b, enc):
        ex.drain()
    for copy in pair + pair_back:
        copy.wait_send()


def local(
    obs_values, kernels, block_owner, block_row, valid_count, enc_weight, enc_bias, conv_weight, cotangent
):
    members = lax.axis_size("wide")
    bits = members.bit_length() - 1
    order_a, order_b = orders(bits)
    blocks, slots, channels = obs_values.shape
    lat_rows, lon, width = cotangent.shape
    half = width // 2
    owner = block_owner[:, 0]
    tile_a = place_of(owner, order_a) * lat_rows + block_row
    tile_b = place_of(owner, order_b) * lat_rows + block_row
    bias = enc_bias.reshape(1, width)
    lat = members * lat_rows
    smem, vmem = pl.BlockSpec(memory_space=pltpu.SMEM), pl.BlockSpec(memory_space=pltpu.VMEM)
    anywhere = pl.BlockSpec(memory_space=pl.ANY)

    dense_a, dense_b = pl.pallas_call(
        encode_kernel,
        out_shape=[jax.ShapeDtypeStruct((lat, lon, half), BF16)] * 2,
        in_specs=[smem] * 3 + [vmem] * 4,
        out_specs=[vmem] * 2,
        scratch_shapes=[pltpu.VMEM((lat, lon, half), F32)] * 2,
        compiler_params=pltpu.CompilerParams(vmem_limit_bytes=58 * MIB),
        name="encode",
    )(tile_a, tile_b, valid_count, obs_values, kernels, enc_weight, bias)

    rows = lat_rows * lon
    keep_slope = lat <= 256
    unit = 16 * members
    conv_rows = -(-3 * width // unit) * unit
    enc_rows = -(-2 * channels // unit) * unit
    grid_rows = members * rows

    def buffers(total):
        return [pltpu.VMEM((total >> (k + 1), half), BF16) for k in range(bits)]

    held = F32 if keep_slope else BF16
    levels = [(low, 1 << min(2, bits - low)) for low in range(0, bits, 2)]
    copies = 8 * bits + 2 * sum(ways - 1 for _, ways in levels) + 4
    scratch = [
        *[pltpu.VMEM((grid_rows // 2, half), BF16)] * 2,
        *[pltpu.VMEM((grid_rows, half), BF16)] * 2,
        pltpu.VMEM((blocks if keep_slope else 1, slots, width), F32),
        *[pltpu.VMEM((rows + 2 * lon, width), BF16)] * 2,
        *[pltpu.VMEM((conv_rows, half), held)] * 2,
        *[pltpu.VMEM((conv_rows // 2, half), BF16)] * 2,
        *[pltpu.VMEM((conv_rows, half), BF16)] * 2,
        pltpu.VMEM((enc_rows, half), F32),
        pltpu.VMEM((enc_rows, half), BF16),
        pltpu.VMEM((channels, width), F32),
        *([pltpu.VMEM((grid_rows // 2, half), F32)] * 2 if keep_slope else []),
        *buffers(grid_rows),
        *buffers(grid_rows),
        *buffers(conv_rows),
        *buffers(conv_rows),
        *[pltpu.VMEM((enc_rows >> low, half), BF16) for low, _ in levels],
        *[pltpu.VMEM((ways - 1, (enc_rows >> low) // ways, half), BF16) for low, ways in levels],
        pltpu.SemaphoreType.DMA((2,)),
        pltpu.SemaphoreType.DMA((copies,)),
        pltpu.SemaphoreType.DMA((copies,)),
    ]
    grid_out, conv_sum, enc_sum = pl.pallas_call(
        functools.partial(grid_kernel, members, keep_slope),
        out_shape=[
            jax.ShapeDtypeStruct((rows, width), BF16),
            jax.ShapeDtypeStruct((3 * width, width), BF16),
            jax.ShapeDtypeStruct((channels, width), BF16),
        ],
        in_specs=[smem] * 3 + [anywhere] * 2 + [vmem] * 6,
        out_specs=[vmem] * 3,
        scratch_shapes=scratch,
        compiler_params=pltpu.CompilerParams(
            collective_id=0, has_side_effects=True, vmem_limit_bytes=60 * MIB
        ),
        name="grid",
    )(
        tile_a,
        tile_b,
        valid_count,
        dense_a.reshape(grid_rows, half),
        dense_b.reshape(grid_rows, half),
        obs_values,
        kernels,
        enc_weight,
        bias,
        conv_weight,
        cotangent.reshape(rows, width),
    )
    return (
        grid_out.reshape(cotangent.shape),
        enc_sum.astype(F32),
        conv_sum.astype(F32).reshape(3, width, width),
    )


def solution(mesh):
    in_specs = (
        P(("groups", "wide"), None, None),
        P(("groups", "wide"), None, None),
        P(("groups", "wide"), None),
        P(("groups", "wide")),
        P(("groups", "wide")),
        P(),
        P(),
        P(),
        P(("groups", "wide"), None, None),
    )
    out_specs = (P(("groups", "wide"), None, None), P("groups", None), P("groups", None, None))
    return jax.shard_map(local, mesh=mesh, in_specs=in_specs, out_specs=out_specs, check_vma=False)
```

```python
import functools
import math

import jax
import jax.numpy as jnp
from jax import lax
from jax.experimental import pallas as pl
from jax.experimental.pallas import tpu as pltpu
from jax.sharding import PartitionSpec as P

F32, BF16 = jnp.float32, jnp.bfloat16
MIB = 1 << 20
ROOT = math.sqrt(2.0 / math.pi)
CUBE = 0.044715


def gelu(x):
    half = 0.5 * x
    return half + half * jnp.tanh(x * (ROOT + (ROOT * CUBE) * (x * x)))


def gelu_slope(x):
    square = x * x
    t = jnp.tanh(x * (ROOT + (ROOT * CUBE) * square))
    bend = x * (0.5 * ROOT + (1.5 * CUBE * ROOT) * square)
    return 0.5 + 0.5 * t + bend * (1.0 - t * t)


def dot(left, right, contract=((1,), (0,))):
    return lax.dot_general(left, right, (contract, ((), ())), preferred_element_type=F32)


def orders(bits):
    plain = list(range(bits))
    other = [plain[0], *plain[2:3], *plain[1:2], *plain[3:]]
    return plain, other


def place_of(index, order):
    place = 0
    for bit in order:
        place = place * 2 + index // (1 << bit) % 2
    return place


def live_part(kern, count):
    live = lax.broadcasted_iota(jnp.int32, kern.shape, 1) < count
    return jnp.where(live, kern, jnp.zeros_like(kern))


def encode_kernel(tile_a, tile_b, count, obs, kern, weight, bias, out_a, out_b, acc_a, acc_b):
    blocks, slots, channels = obs.shape
    half = out_a.shape[-1]
    rows = acc_a.shape[0]

    @pl.loop(0, rows, unroll=4)
    def _(r):
        acc_a[r] = jnp.zeros(acc_a.shape[1:], F32)
        acc_b[r] = jnp.zeros(acc_b.shape[1:], F32)

    @pl.loop(0, blocks // 4)
    def _(i):
        for j in range(4):
            b = i * 4 + j
            pre = dot(obs[b], weight[...]) + bias[...]
            hidden = gelu(pre).astype(BF16)
            contrib = dot(live_part(kern[b], count[b]), hidden).astype(BF16).astype(F32)
            acc_a[tile_a[b]] += contrib[:, :half]
            acc_b[tile_b[b]] += contrib[:, half:]

    @pl.loop(0, rows, unroll=4)
    def _(r):
        out_a[r] = acc_a[r].astype(BF16)
        out_b[r] = acc_b[r].astype(BF16)


class Exchange:
    def __init__(self, order, total, me, copies):
        self.me, self.copies = me, copies
        self.partner, self.keep, self.give, self.size = [], [], [], []
        base, size = 0, total
        for bit in order:
            mine = me // (1 << bit) % 2
            size = size // 2
            self.partner.append(me + (1 - 2 * mine) * (1 << bit))
            self.keep.append(base + mine * size)
            self.give.append(base + (1 - mine) * size)
            self.size.append(size)
            base = base + mine * size
        self.pending = {}

    def region(self, ref, offset, size):
        return ref.at[pl.ds(pl.multiple_of(offset, 16), size)]

    def send(self, src, dst, k, tag):
        self.pending[(tag, k)] = self.copies(src, dst, self.partner[k])

    def start_sum(self, k, source, recv, shift=0):
        self.send(self.region(source, self.give[k] - shift, self.size[k]), recv[k], k, "s")

    def start_rounded(self, source, stage, recv):
        self.add(stage, 0, [(source, self.give[0])], self.size[0])
        self.send(stage, recv[0], 0, "s")

    @staticmethod
    def add(out, at, terms, size):
        step = math.gcd(size, 256)

        @pl.loop(0, size // step)
        def _(i):
            parts = [
                ref[pl.ds(pl.multiple_of(start + i * step, 16), step)].astype(F32)
                for ref, start in terms
            ]
            place = pl.ds(pl.multiple_of(at + i * step, 16), step)
            out[place] = sum(parts[1:], parts[0]).astype(out.dtype)

    def finish_sum(self, k, source, out, recv, shift=0):
        self.pending[("s", k)].wait_recv()
        base, keep, size = self.keep[k], self.keep[k], self.size[k]
        if ("s", k) != ("s", len(self.size) - 1):
            give, keep, size = self.give[k + 1], self.keep[k + 1], self.size[k + 1]
            self.add(recv[k], give - base, [(source, give - shift), (recv[k], give - base)], size)
            self.send(self.region(recv[k], give - base, size), recv[k + 1], k + 1, "s")
        self.add(out, keep - shift, [(source, keep - shift), (recv[k], keep - base)], size)

    def start_gather(self, k, buffer):
        where = self.region(buffer, self.keep[k], self.size[k])
        self.send(where, where, k, "g")

    def finish_gather(self, k):
        self.pending[("g", k)].wait_recv()

    def drain(self):
        for copy in self.pending.values():
            copy.wait_send()


class ShortExchange:
    def __init__(self, bits, total, me, copies):
        self.copies, self.sent, self.levels = copies, [], []
        base, size = 0, total
        for low in range(0, bits, 2):
            unit, ways = 1 << low, 1 << min(2, bits - low)
            digit = me // unit % ways
            size = size // ways
            others = [lax.rem(digit + d, ways) for d in range(1, ways)]
            peers = [(other, me + (other - digit) * unit) for other in others]
            self.levels.append((base, digit, size, peers))
            base = base + digit * size
        self.base, self.size = base, size

    def peers(self):
        return [peer for level in self.levels for _, peer in level[3]]

    def sum(self, k, work, stage, recv):
        base, digit, size, peers = self.levels[k]
        Exchange.add(stage[k], 0, [(work, base)], size * (len(peers) + 1))
        pending = [
            self.copies(stage[k].at[pl.ds(pl.multiple_of(other * size, 16), size)], recv[k].at[d], peer)
            for d, (other, peer) in enumerate(peers)
        ]
        self.sent += pending
        mine = pl.ds(pl.multiple_of(base + digit * size, 16), size)
        for copy in pending:
            copy.wait_recv()
        total = work[mine]
        for d in range(len(peers)):
            total = total + recv[k][d].astype(F32)
        work[mine] = total

    def gather(self, k, buffer):
        base, digit, size, peers = self.levels[k]
        mine = buffer.at[pl.ds(pl.multiple_of(base + digit * size, 16), size)]
        pending = [self.copies(mine, mine, peer) for _, peer in peers]
        self.sent += pending
        for copy in pending:
            copy.wait_recv()

    def drain(self):
        for copy in self.sent:
            copy.wait_send()


def grid_kernel(
    members,
    keep_slope,
    tile_a,
    tile_b,
    count,
    dense_a,
    dense_b,
    obs,
    kern,
    weight,
    bias,
    conv_weight,
    cotangent,
    grid_out,
    conv_out,
    enc_out,
    *scratch,
):
    scratch = list(scratch)
    bits = members.bit_length() - 1
    order_a, order_b = orders(bits)
    send_sems, recv_sems, local_sems = scratch.pop(), scratch.pop(), scratch.pop()
    work_a, work_b, gb_a, gb_b, slope, grid_pad, back_pad, cw_a, cw_b, cs_a, cs_b, cg_a, cg_b, ew, eg, total = scratch[:16]
    acc_a, acc_b = scratch[16:18] if keep_slope else (work_a, work_b)
    rest = scratch[18:] if keep_slope else scratch[16:]
    recv_a, recv_b, crecv_a, crecv_b = [rest[i * bits : (i + 1) * bits] for i in range(4)]
    levels = (bits + 1) // 2
    estage, erecv = rest[4 * bits : 4 * bits + levels], rest[4 * bits + levels :]

    blocks, slots, channels = obs.shape
    lon = kern.shape[1]
    rows, width = cotangent.shape
    half = width // 2
    me = lax.axis_index("wide")

    used = [0]

    def copies(src, dst, target):
        at = used[0]
        used[0] += 1
        copy = pltpu.make_async_remote_copy(
            src_ref=src,
            dst_ref=dst,
            send_sem=send_sems.at[at],
            recv_sem=recv_sems.at[at],
            device_id={"wide": target},
            device_id_type=pl.DeviceIdType.MESH,
        )
        copy.start()
        return copy

    after, before = lax.rem(me + 1, members), lax.rem(me + members - 1, members)
    grid_rows = members * rows
    sum_a, sum_b = Exchange(order_a, grid_rows, me, copies), Exchange(order_b, grid_rows, me, copies)
    conv_a, conv_b = Exchange(order_a, cw_a.shape[0], me, copies), Exchange(order_b, cw_b.shape[0], me, copies)
    enc = ShortExchange(bits, ew.shape[0], me, copies)

    barrier = pltpu.get_barrier_semaphore()
    greeted = [before, after, *enc.peers()]
    for peer in greeted:
        pl.semaphore_signal(barrier, inc=1, device_id={"wide": peer}, device_id_type=pl.DeviceIdType.MESH)
    pl.semaphore_wait(barrier, len(greeted))

    def slope_of(b):
        pre = dot(obs[b], weight[...]) + bias[...]
        return gelu_slope(pre)

    def fill_slope(low, high):
        if keep_slope:

            @pl.loop(low, high)
            def _(b):
                slope[b] = slope_of(b)

    streams = ((sum_a, dense_a, work_a, recv_a, gb_a), (sum_b, dense_b, work_b, recv_b, gb_b))
    sums = (acc_a, acc_b)
    local = []
    for n, (ex, dense, work, recv, _) in enumerate(streams):
        ex.start_sum(0, dense, recv)
        local.append(
            pltpu.make_async_copy(ex.region(dense, ex.keep[0], ex.size[0]), work, local_sems.at[n])
        )
        local[-1].start()
    cuts = [blocks * k // bits for k in range(bits + 1)]
    fill_slope(cuts[0], cuts[1])
    for k in range(bits):
        for n, (ex, dense, work, recv, _) in enumerate(streams):
            shift = ex.keep[0]
            if k == 0:
                local[n].wait()
            ex.finish_sum(k, work if k == 0 else sums[n], sums[n], recv, shift)
        if k + 1 < bits:
            fill_slope(cuts[k + 1], cuts[k + 2])

    own = pl.ds(lon, rows)
    for n, (ex, dense, work, recv, _) in enumerate(streams):
        mine = pl.ds(pl.multiple_of(ex.keep[-1] - ex.keep[0], 16), rows)
        grid_pad[own, n * half : (n + 1) * half] = sums[n][mine].astype(BF16)

    def halo(pad):
        up = copies(pad.at[pl.ds(rows, lon)], pad.at[pl.ds(0, lon)], after)
        down = copies(pad.at[pl.ds(lon, lon)], pad.at[pl.ds(lon + rows, lon)], before)
        return up, down

    def landed(pad, pair):
        for copy in pair:
            copy.wait_recv()
        first, last = pl.ds(0, lon), pl.ds(lon + rows, lon)
        nothing = jnp.zeros((lon, width), BF16)
        pad[first] = jnp.where(me == 0, nothing, pad[first])
        pad[last] = jnp.where(me == members - 1, nothing, pad[last])

    above, below = pl.ds(0, rows), pl.ds(2 * lon, rows)
    pair = halo(grid_pad)
    conv_in = dot(grid_pad[own], conv_weight[1])
    landed(grid_pad, pair)
    conv_in = conv_in + dot(grid_pad[above], conv_weight[0]) + dot(grid_pad[below], conv_weight[2])
    back_pad[own] = (cotangent[...].astype(F32) * gelu_slope(conv_in)).astype(BF16)
    pair_back = halo(back_pad)
    grid_out[...] = (grid_pad[own].astype(F32) + gelu(conv_in)).astype(BF16)
    turned = ((1,), (1,))
    grid_back = cotangent[...].astype(F32) + dot(back_pad[own], conv_weight[1], turned)
    landed(back_pad, pair_back)
    grid_back = grid_back + dot(back_pad[below], conv_weight[0], turned)
    grid_back = (grid_back + dot(back_pad[above], conv_weight[2], turned)).astype(BF16)
    for n, (ex, _, _, _, gb) in enumerate(streams):
        gb[pl.ds(pl.multiple_of(ex.keep[-1], 16), rows)] = grid_back[:, n * half : (n + 1) * half]
        ex.start_gather(bits - 1, gb)

    outer = ((0,), (0,))
    used_rows = 3 * width
    for k, place in enumerate((above, own, below)):
        term = dot(grid_pad[place], back_pad[own], outer).astype(cw_a.dtype)
        cw_a[k * width : (k + 1) * width] = term[:, :half]
        cw_b[k * width : (k + 1) * width] = term[:, half:]
    if cw_a.shape[0] > used_rows:
        cw_a[used_rows:] = jnp.zeros((cw_a.shape[0] - used_rows, half), cw_a.dtype)
        cw_b[used_rows:] = jnp.zeros((cw_b.shape[0] - used_rows, half), cw_b.dtype)
    conv_streams = ((conv_a, cw_a, crecv_a, cg_a), (conv_b, cw_b, crecv_b, cg_b))
    for (ex, cw, recv, _), stage in zip(conv_streams, (cs_a, cs_b)):
        ex.start_rounded(cw, stage, recv)
    for k in range(bits):
        for ex, _, _, _, gb in streams:
            ex.finish_gather(bits - 1 - k)
            if k + 1 < bits:
                ex.start_gather(bits - 2 - k, gb)
        if k > 0:
            for ex, cw, recv, _ in conv_streams:
                ex.finish_sum(k - 1, cw, cw, recv)

    def conv_step(k):
        for ex, cw, recv, cg in conv_streams:
            if k == 0:
                ex.finish_sum(bits - 1, cw, cw, recv)
                mine = pl.ds(pl.multiple_of(ex.keep[-1], 16), ex.size[-1])
                cg[mine] = cw[mine].astype(BF16)
            else:
                ex.finish_gather(bits - k)
            if k < bits:
                ex.start_gather(bits - 1 - k, cg)

    total[...] = jnp.zeros_like(total)

    def encoder_steps(low, high):
        @pl.loop(low, high)
        def _(i):
            parts = []
            for j in range(2):
                b = i * 2 + j
                tile = jnp.concatenate([gb_a3[tile_a[b]], gb_b3[tile_b[b]]], axis=-1)
                hidden_back = dot(live_part(kern[b], count[b]), tile, outer)
                factor = slope[b] if keep_slope else slope_of(b)
                parts.append((hidden_back * factor).astype(BF16))
            pair_obs = obs[pl.ds(i * 2, 2)].reshape(2 * slots, channels)
            total[...] += dot(pair_obs, jnp.concatenate(parts, axis=0), outer)

    gb_a3 = gb_a.reshape(grid_rows // lon, lon, half)
    gb_b3 = gb_b.reshape(grid_rows // lon, lon, half)
    cuts = [blocks // 2 * k // bits for k in range(bits + 1)]
    done = 0
    for k in range(bits):
        encoder_steps(cuts[k], cuts[k + 1])
        if k in (bits // 2, bits - 1):
            conv_step(done)
            done += 1
    ew[:channels] = total[:, :half]
    ew[channels : 2 * channels] = total[:, half:]
    if ew.shape[0] > 2 * channels:
        ew[2 * channels :] = jnp.zeros((ew.shape[0] - 2 * channels, half), F32)
    for k in range(levels):
        enc.sum(k, ew, estage, erecv)
        if done <= bits:
            conv_step(done)
            done += 1
    mine = pl.ds(pl.multiple_of(enc.base, 16), enc.size)
    eg[mine] = ew[mine].astype(BF16)
    for k in range(levels):
        enc.gather(levels - 1 - k, eg)
        if done <= bits:
            conv_step(done)
            done += 1
    while done <= bits:
        conv_step(done)
        done += 1
    conv_out[:, :half] = cg_a[:used_rows]
    conv_out[:, half:] = cg_b[:used_rows]
    enc_out[:, :half] = eg[:channels]
    enc_out[:, half:] = eg[channels : 2 * channels]
    for ex in (sum_a, sum_b, conv_a, conv_b, enc):
        ex.drain()
    for copy in pair + pair_back:
        copy.wait_send()


def local(
    obs_values, kernels, block_owner, block_row, valid_count, enc_weight, enc_bias, conv_weight, cotangent
):
    members = lax.axis_size("wide")
    bits = members.bit_length() - 1
    order_a, order_b = orders(bits)
    blocks, slots, channels = obs_values.shape
    lat_rows, lon, width = cotangent.shape
    half = width // 2
    owner = block_owner[:, 0]
    tile_a = place_of(owner, order_a) * lat_rows + block_row
    tile_b = place_of(owner, order_b) * lat_rows + block_row
    bias = enc_bias.reshape(1, width)
    lat = members * lat_rows
    smem, vmem = pl.BlockSpec(memory_space=pltpu.SMEM), pl.BlockSpec(memory_space=pltpu.VMEM)
    anywhere = pl.BlockSpec(memory_space=pl.ANY)

    dense_a, dense_b = pl.pallas_call(
        encode_kernel,
        out_shape=[jax.ShapeDtypeStruct((lat, lon, half), BF16)] * 2,
        in_specs=[smem] * 3 + [vmem] * 4,
        out_specs=[vmem] * 2,
        scratch_shapes=[pltpu.VMEM((lat, lon, half), F32)] * 2,
        compiler_params=pltpu.CompilerParams(vmem_limit_bytes=58 * MIB),
        name="encode",
    )(tile_a, tile_b, valid_count, obs_values, kernels, enc_weight, bias)

    rows = lat_rows * lon
    keep_slope = lat <= 256
    unit = 16 * members
    conv_rows = -(-3 * width // unit) * unit
    enc_rows = -(-2 * channels // unit) * unit
    grid_rows = members * rows

    def buffers(total):
        return [pltpu.VMEM((total >> (k + 1), half), BF16) for k in range(bits)]

    held = F32 if keep_slope else BF16
    levels = [(low, 1 << min(2, bits - low)) for low in range(0, bits, 2)]
    copies = 8 * bits + 2 * sum(ways - 1 for _, ways in levels) + 4
    scratch = [
        *[pltpu.VMEM((grid_rows // 2, half), BF16)] * 2,
        *[pltpu.VMEM((grid_rows, half), BF16)] * 2,
        pltpu.VMEM((blocks if keep_slope else 1, slots, width), F32),
        *[pltpu.VMEM((rows + 2 * lon, width), BF16)] * 2,
        *[pltpu.VMEM((conv_rows, half), held)] * 2,
        *[pltpu.VMEM((conv_rows // 2, half), BF16)] * 2,
        *[pltpu.VMEM((conv_rows, half), BF16)] * 2,
        pltpu.VMEM((enc_rows, half), F32),
        pltpu.VMEM((enc_rows, half), BF16),
        pltpu.VMEM((channels, width), F32),
        *([pltpu.VMEM((grid_rows // 2, half), F32)] * 2 if keep_slope else []),
        *buffers(grid_rows),
        *buffers(grid_rows),
        *buffers(conv_rows),
        *buffers(conv_rows),
        *[pltpu.VMEM((enc_rows >> low, half), BF16) for low, _ in levels],
        *[pltpu.VMEM((ways - 1, (enc_rows >> low) // ways, half), BF16) for low, ways in levels],
        pltpu.SemaphoreType.DMA((2,)),
        pltpu.SemaphoreType.DMA((copies,)),
        pltpu.SemaphoreType.DMA((copies,)),
    ]
    grid_out, conv_sum, enc_sum = pl.pallas_call(
        functools.partial(grid_kernel, members, keep_slope),
        out_shape=[
            jax.ShapeDtypeStruct((rows, width), BF16),
            jax.ShapeDtypeStruct((3 * width, width), BF16),
            jax.ShapeDtypeStruct((channels, width), BF16),
        ],
        in_specs=[smem] * 3 + [anywhere] * 2 + [vmem] * 6,
        out_specs=[vmem] * 3,
        scratch_shapes=scratch,
        compiler_params=pltpu.CompilerParams(
            collective_id=0, has_side_effects=True, vmem_limit_bytes=60 * MIB
        ),
        name="grid",
    )(
        tile_a,
        tile_b,
        valid_count,
        dense_a.reshape(grid_rows, half),
        dense_b.reshape(grid_rows, half),
        obs_values,
        kernels,
        enc_weight,
        bias,
        conv_weight,
        cotangent.reshape(rows, width),
    )
    return (
        grid_out.reshape(cotangent.shape),
        enc_sum.astype(F32),
        conv_sum.astype(F32).reshape(3, width, width),
    )


def solution(mesh):
    in_specs = (
        P(("groups", "wide"), None, None),
        P(("groups", "wide"), None, None),
        P(("groups", "wide"), None),
        P(("groups", "wide")),
        P(("groups", "wide")),
        P(),
        P(),
        P(),
        P(("groups", "wide"), None, None),
    )
    out_specs = (P(("groups", "wide"), None, None), P("groups", None), P("groups", None, None))
    return jax.shard_map(local, mesh=mesh, in_specs=in_specs, out_specs=out_specs, check_vma=False)
```
